32 devices in a mesh: frag: 2 (over x), tile: 16 (over z, y, core).
Axes of the slice: x: 2, y: 2, z: 4, core: 2. Of those that a mesh axis runs over, the one named last changes fastest.
Arguments:
- amps: bfloat16 [32, 16, 16, 1024], P(('frag', 'tile')), parts along dimension 0, may hold values from -6 to 6
- ladder_ints: bfloat16 [32, 1024, 1024], P(('frag', 'tile')), parts along dimension 0, may hold values from -0.1875 to 0.1875
- quad_pairs: int32 [32, 2], P(('frag', 'tile')), parts along dimension 0, may hold values from 0 to 15, as said below
- cycle_ints: bfloat16 [4096, 2048], P(('frag', 'tile')), parts along dimension 0, may hold values from -0.125 to 0.125
Outputs:
- residual: bfloat16 [32, 16, 16, 1024], P('frag', 'tile'), parts along dimension 0
The draws below stay inside these ranges and needn't reach their ends.
There are 2 independent parts, one for each index of `frag`. The reference program is written for one: setup_inputs(seed, part) draws one part's arguments, and reference() takes and returns one part's arrays. A program takes and returns all parts, laid end to end along the dimension named above; each array names one. Nothing has to cross between parts.
Inputs may be any that keep to these rules, and one draw needn't show every extreme that they name: `quad_pairs`: each row names an output tile pair and an input tile pair; no two rows are equal; every tile pair is named as output by some row and as input by some row; each device holds 1 row and the matching integral tiles.
All inputs are finite; a program needn't handle non-finite values.
Results may differ from the reference program's by a relative error of at most 0.0053.
Values may be sent and summed in bfloat16 or wider, within the bound.
No kernel may reach another device: no remote copies, remote signals or barrier semaphores. Data moves between devices by JAX's collectives and lax.ppermute only.
A program may use at most 128 MiB of HBM per device.

```python
import jax
import jax.numpy as jnp
from jax import lax

TS = 32
VT = 4
OCC = 16
NTP = 16
TSQ = 1024
NQ = 16
ROWS = 2048


def draw_quad_pairs(key, part):
    key = jax.random.fold_in(key, 7)
    first, second, third = jax.random.split(key, 3)
    out_order = jax.random.permutation(first, NTP).astype(jnp.int32)
    in_order = jax.random.permutation(second, NTP).astype(jnp.int32)
    row_order = jax.random.permutation(third, NQ).astype(jnp.int32)
    counter = jnp.arange(NQ, dtype=jnp.int32)
    lower = counter % NTP
    upper = counter // NTP
    rows = jnp.stack([out_order[lower], in_order[(lower + upper) % NTP]], axis=1).astype(jnp.int32)
    return rows[row_order]


def level_of(own_key, shape, shards, low, largest):
    level, own = 1.0, jax.random.fold_in(own_key, 6)
    for position, shards_of in shards:
        heights = jnp.exp(jax.random.uniform(jax.random.fold_in(own, position), (shards_of,), jnp.float32, low / len(shards), largest / len(shards)))
        level = level * jnp.repeat(heights, shape[position] // shards_of).reshape([-1 if axis == position else 1 for axis in range(len(shape))])
    return level


def centred(stream_key, shape, width, reach, shards=(), kind=jnp.bfloat16):
    array = width * jax.random.normal(stream_key, shape, jnp.float32)
    if shards:
        array = array * level_of(stream_key, shape, shards, -0.22, 0.18)
    return jnp.clip(array, -reach, reach).astype(kind)


def setup_inputs(seed: int = 0, part: int = 0) -> dict:
    splits = jax.random.split(jax.random.key(seed), 5)
    own_keys = jax.random.split(jax.random.fold_in(splits[4], part), 5)
    return {
        "amps": centred(own_keys[0], (OCC, OCC, NTP, TSQ), 1.0, 6.0, ((0, 16),)),
        "ladder_ints": centred(own_keys[1], (NQ, TSQ, TSQ), TSQ ** -0.5, 0.1875, ((0, 16),)),
        "quad_pairs": draw_quad_pairs(jax.random.fold_in(jax.random.fold_in(splits[4], part), 71), part),
        "cycle_ints": centred(own_keys[3], (ROWS, ROWS), ROWS ** -0.5, 0.125, ((0, 16),)),
    }


def reference(amps, ladder_ints, quad_pairs, cycle_ints):
    flat = amps.reshape(OCC * OCC, NTP, TSQ)
    tile_ids = jnp.arange(NTP, dtype=jnp.int32)

    def accumulate(index, total):
        out_tile = quad_pairs[index, 0]
        in_tile = quad_pairs[index, 1]
        column = lax.dynamic_index_in_dim(flat, in_tile, 1, keepdims=False)
        partial_value = jnp.dot(column, ladder_ints[index], preferred_element_type=jnp.float32).astype(jnp.bfloat16)
        partial_value = lax.optimization_barrier(partial_value).astype(jnp.float32)
        select = (tile_ids == out_tile).astype(jnp.float32)
        return total + select[None, :, None] * partial_value[:, None, :]

    ladder = lax.fori_loop(0, NQ, accumulate, jnp.zeros((OCC * OCC, NTP, TSQ), jnp.float32))
    ladder = ladder.reshape(OCC, OCC, NTP, TSQ)
    updated = (amps.astype(jnp.float32) + ladder).astype(jnp.bfloat16)
    cycle_input = updated.reshape(OCC, OCC, VT, VT, TS, TS).transpose(0, 2, 4, 1, 3, 5).reshape(ROWS, ROWS)
    cycle = jnp.dot(cycle_ints, cycle_input, preferred_element_type=jnp.float32)
    cycle = cycle.reshape(OCC, VT, TS, OCC, VT, TS).transpose(0, 3, 1, 4, 2, 5).reshape(OCC, OCC, NTP, TSQ)
    return (ladder + cycle).astype(jnp.bfloat16)
```

```python
import functools

import jax
import jax.numpy as jnp
from jax import lax
from jax.experimental import pallas as pl
from jax.experimental.pallas import tpu as pltpu
from jax.sharding import PartitionSpec as P

TS = 32
VT = 4
NTP = VT * VT
LANES = 128
GROUPS = LANES // TS
STRIPES = TS // GROUPS


def swap_groups(four):
    lane = lax.broadcasted_iota(jnp.int32, four[0].shape, four[0].ndim - 1)
    low = lane < 2 * TS
    even = (lane // TS) % 2 == 0
    v = list(four)
    for p in (0, 1):
        a, b = v[p], v[p + 2]
        v[p] = jnp.where(low, a, pltpu.roll(b, 2 * TS, 1))
        v[p + 2] = jnp.where(low, pltpu.roll(a, 2 * TS, 1), b)
    for p in (0, 2):
        a, b = v[p], v[p + 1]
        v[p] = jnp.where(even, a, pltpu.roll(b, TS, 1))
        v[p + 1] = jnp.where(even, pltpu.roll(a, LANES - TS, 1), b)
    return v


def finish_kernel(places, targets, part_ref, amp_ref, *rest):
    places, copied = places
    pieces = rest[:copied]
    out_ref, matrix, ladder, columns, product, result, sems = rest[copied:]
    occ = amp_ref.shape[1]
    spread = VT * TS

    copies = []
    for n, piece in enumerate(pieces):
        rows = piece.shape[0]
        start = pl.multiple_of(places[n] * rows, rows)
        copy = pltpu.make_async_copy(piece, matrix.at[pl.ds(start, rows)], sems.at[n])
        copy.start()
        copies.append(copy)

    if part_ref.shape[0] == NTP:
        for q in range(part_ref.shape[0]):
            ladder[targets[q]] = part_ref[q].astype(jnp.float32)
    else:
        ladder[...] = jnp.zeros_like(ladder)
        for q in range(part_ref.shape[0]):
            ladder[targets[q]] += part_ref[q].astype(jnp.float32)

    for C in range(VT):
        for h in range(STRIPES):
            lanes = slice(h * LANES, (h + 1) * LANES)
            four = []
            for B in range(VT):
                pair = C * VT + B
                total = amp_ref[pair, :, lanes].astype(jnp.float32) + ladder[pair, :, lanes]
                four.append(total)
            for g, value in enumerate(swap_groups(four)):
                columns[pl.ds(C * TS + h * GROUPS + g, occ, stride=spread), :] = value
    right = columns[...].astype(jnp.bfloat16)

    for copy in copies:
        copy.wait()
    step = min(512, matrix.shape[0])
    for r in range(0, matrix.shape[0], step):
        product[r:r + step, :] = jnp.dot(
            matrix[r:r + step, :], right, preferred_element_type=jnp.float32
        )

    for A in range(VT):
        for h in range(STRIPES):
            lanes = slice(h * LANES, (h + 1) * LANES)
            four = [
                product[pl.ds(A * TS + h * GROUPS + g, occ, stride=spread), :]
                for g in range(GROUPS)
            ]
            for B, value in enumerate(swap_groups(four)):
                pair = A * VT + B
                result[h, pl.ds(pair, occ, stride=NTP), :] = value + ladder[pair, :, lanes]
    for h in range(STRIPES):
        lanes = slice(h * LANES, (h + 1) * LANES)
        out_ref[:, :, lanes] = result[h].astype(jnp.bfloat16).reshape(occ, NTP, LANES)


def finish(places, targets, part, amp, pieces):
    occ = amp.shape[1]
    rows = occ * VT * TS

    def kernel(places_ref, targets_ref, *refs):
        finish_kernel((places_ref, len(pieces)), targets_ref, *refs)

    whole = pl.BlockSpec(memory_space=pltpu.VMEM)
    scalars = pl.BlockSpec(memory_space=pltpu.SMEM)
    return pl.pallas_call(
        kernel,
        out_shape=jax.ShapeDtypeStruct((occ, NTP, TS * TS), jnp.bfloat16),
        in_specs=[scalars, scalars, whole, whole]
        + [pl.BlockSpec(memory_space=pl.ANY)] * len(pieces),
        out_specs=whole,
        scratch_shapes=[
            pltpu.VMEM((rows, rows), jnp.bfloat16),
            pltpu.VMEM((NTP, occ, TS * TS), jnp.float32),
            pltpu.VMEM((rows, VT * TS), jnp.float32),
            pltpu.VMEM((rows, VT * TS), jnp.float32),
            pltpu.VMEM((STRIPES, occ * NTP, LANES), jnp.float32),
            pltpu.SemaphoreType.DMA((len(pieces),)),
        ],
        compiler_params=pltpu.CompilerParams(vmem_limit_bytes=56 * 1024 * 1024),
        cost_estimate=pl.CostEstimate(
            flops=2 * rows * rows * VT * TS,
            bytes_accessed=2 * rows * rows,
            transcendentals=0,
        ),
    )(places, targets, part, amp, *pieces)


def ladder_kernel(arrived_ref, ints_ref, out_ref, total):
    occ = out_ref.shape[0]
    value = jnp.dot(
        arrived_ref[...].reshape(occ * occ, TS * TS),
        ints_ref[0],
        preferred_element_type=jnp.float32,
    )
    for h in range(STRIPES):
        lanes = slice(h * LANES, (h + 1) * LANES)
        total[h] = value[:, lanes]
        for j in range(occ):
            out_ref[j, :, lanes] = total[h, pl.ds(j, occ, stride=occ), :].astype(jnp.bfloat16)


def ladder_partial(arrived, ladder_ints):
    occ = arrived.shape[0]
    whole = pl.BlockSpec(memory_space=pltpu.VMEM)
    return pl.pallas_call(
        ladder_kernel,
        out_shape=jax.ShapeDtypeStruct((occ, occ, TS * TS), jnp.bfloat16),
        in_specs=[whole, whole],
        out_specs=whole,
        scratch_shapes=[pltpu.VMEM((STRIPES, occ * occ, LANES), jnp.float32)],
        compiler_params=pltpu.CompilerParams(vmem_limit_bytes=40 * 1024 * 1024),
        cost_estimate=pl.CostEstimate(
            flops=2 * occ * occ * TS**4, bytes_accessed=2 * TS**4, transcendentals=0
        ),
    )(arrived, ladder_ints)


def per_device(amps, ladder_ints, quad_pairs, cycle_ints):
    members = lax.axis_size("tile")
    occ = amps.shape[1]
    swap = functools.partial(lax.all_to_all, axis_name="tile", tiled=True)
    matrix = lax.all_gather(cycle_ints, "tile", axis=0, tiled=True)
    tags = jnp.broadcast_to(
        jnp.repeat(quad_pairs.astype(jnp.bfloat16), LANES // 2, axis=1)[:, None, :],
        (occ, NTP, LANES),
    )
    sent = jnp.concatenate([amps[0], tags], axis=2)
    moved = swap(sent, split_axis=0, concat_axis=0)
    pairs = moved[:, 0, TS * TS:].astype(jnp.int32)
    targets, inputs = pairs[:, 0], pairs[:, LANES // 2]
    amp_cycle = moved[:, :, :TS * TS].transpose(1, 0, 2)
    tiles = amps[0].transpose(1, 0, 2)
    wanted = jnp.take(tiles, inputs, axis=0, mode="clip")
    arrived = swap(wanted, split_axis=0, concat_axis=0)
    partial_value = ladder_partial(arrived, ladder_ints)
    part_moved = swap(partial_value, split_axis=0, concat_axis=0)
    residual = finish(jnp.zeros((1,), jnp.int32), targets, part_moved, amp_cycle, [matrix])
    return residual[:, None]


def solution(mesh):
    return jax.shard_map(
        per_device,
        mesh=mesh,
        in_specs=(
            P(("frag", "tile"), None, None, None),
            P(("frag", "tile"), None, None),
            P(("frag", "tile"), None),
            P(("frag", "tile"), None),
        ),
        out_specs=P("frag", "tile", None, None),
        check_vma=False,
    )
```

```python
import functools

import jax
import jax.numpy as jnp
import numpy as np
from jax import lax
from jax.experimental import pallas as pl
from jax.experimental.pallas import tpu as pltpu
from jax.sharding import PartitionSpec as P

TS = 32
VT = 4
NTP = VT * VT
LANES = 128
GROUPS = LANES // TS
STRIPES = TS // GROUPS
SIDES = 2
CORES = 2


def swap_groups(four):
    lane = lax.broadcasted_iota(jnp.int32, four[0].shape, four[0].ndim - 1)
    low = lane < 2 * TS
    even = (lane // TS) % 2 == 0
    v = list(four)
    for p in (0, 1):
        a, b = v[p], v[p + 2]
        v[p] = jnp.where(low, a, pltpu.roll(b, 2 * TS, 1))
        v[p + 2] = jnp.where(low, pltpu.roll(a, 2 * TS, 1), b)
    for p in (0, 2):
        a, b = v[p], v[p + 1]
        v[p] = jnp.where(even, a, pltpu.roll(b, TS, 1))
        v[p + 1] = jnp.where(even, pltpu.roll(a, LANES - TS, 1), b)
    return v


def finish_kernel(places, targets, part_ref, amp_ref, *rest):
    places, copied = places
    pieces = rest[:copied]
    out_ref, ladder, columns, product, result = rest[copied:]
    occ = amp_ref.shape[1]
    spread = VT * TS

    if part_ref.shape[0] == NTP:
        for q in range(part_ref.shape[0]):
            ladder[targets[q]] = part_ref[q].astype(jnp.float32)
    else:
        ladder[...] = jnp.zeros_like(ladder)
        for q in range(part_ref.shape[0]):
            ladder[targets[q]] += part_ref[q].astype(jnp.float32)

    for C in range(VT):
        for h in range(STRIPES):
            lanes = slice(h * LANES, (h + 1) * LANES)
            four = []
            for B in range(VT):
                pair = C * VT + B
                total = amp_ref[pair, :, lanes].astype(jnp.float32) + ladder[pair, :, lanes]
                four.append(total)
            for g, value in enumerate(swap_groups(four)):
                columns[pl.ds(C * TS + h * GROUPS + g, occ, stride=spread), :] = value
    right = columns[...].astype(jnp.bfloat16)

    for n, piece in enumerate(pieces):
        rows = piece.shape[0]
        start = pl.multiple_of(places[n] * rows, rows)
        product[pl.ds(start, rows), :] = jnp.dot(
            piece[...], right, preferred_element_type=jnp.float32
        )

    for A in range(VT):
        for h in range(STRIPES):
            lanes = slice(h * LANES, (h + 1) * LANES)
            four = [
                product[pl.ds(A * TS + h * GROUPS + g, occ, stride=spread), :]
                for g in range(GROUPS)
            ]
            for B, value in enumerate(swap_groups(four)):
                pair = A * VT + B
                result[h, pl.ds(pair, occ, stride=NTP), :] = value + ladder[pair, :, lanes]
    for h in range(STRIPES):
        lanes = slice(h * LANES, (h + 1) * LANES)
        out_ref[:, :, lanes] = result[h].astype(jnp.bfloat16).reshape(occ, NTP, LANES)


def finish(places, targets, part, amp, pieces):
    occ = amp.shape[1]
    rows = occ * VT * TS

    def kernel(places_ref, targets_ref, *refs):
        finish_kernel((places_ref, len(pieces)), targets_ref, *refs)

    whole = pl.BlockSpec(memory_space=pltpu.VMEM)
    scalars = pl.BlockSpec(memory_space=pltpu.SMEM)
    return pl.pallas_call(
        kernel,
        out_shape=jax.ShapeDtypeStruct((occ, NTP, TS * TS), jnp.bfloat16),
        in_specs=[scalars, scalars] + [whole] * (2 + len(pieces)),
        out_specs=whole,
        scratch_shapes=[
            pltpu.VMEM((NTP, occ, TS * TS), jnp.float32),
            pltpu.VMEM((rows, VT * TS), jnp.float32),
            pltpu.VMEM((rows, VT * TS), jnp.float32),
            pltpu.VMEM((STRIPES, occ * NTP, LANES), jnp.float32),
        ],
        compiler_params=pltpu.CompilerParams(
            vmem_limit_bytes=2 * rows * rows + (rows // 128) * 1024 * 1024
        ),
        cost_estimate=pl.CostEstimate(
            flops=2 * rows * rows * VT * TS,
            bytes_accessed=2 * rows * rows,
            transcendentals=0,
        ),
    )(places, targets, part, amp, *pieces)


def ladder_kernel(arrived_ref, ints_ref, out_ref, total):
    occ = out_ref.shape[0]
    value = jnp.dot(
        arrived_ref[...].reshape(occ * occ, TS * TS),
        ints_ref[0],
        preferred_element_type=jnp.float32,
    )
    for h in range(STRIPES):
        lanes = slice(h * LANES, (h + 1) * LANES)
        total[h] = value[:, lanes]
        for j in range(occ):
            out_ref[j, :, lanes] = total[h, pl.ds(j, occ, stride=occ), :].astype(jnp.bfloat16)


def ladder_partial(arrived, ladder_ints):
    occ = arrived.shape[0]
    whole = pl.BlockSpec(memory_space=pltpu.VMEM)
    return pl.pallas_call(
        ladder_kernel,
        out_shape=jax.ShapeDtypeStruct((occ, occ, TS * TS), jnp.bfloat16),
        in_specs=[whole, whole],
        out_specs=whole,
        scratch_shapes=[pltpu.VMEM((STRIPES, occ * occ, LANES), jnp.float32)],
        compiler_params=pltpu.CompilerParams(vmem_limit_bytes=20 * 1024 * 1024),
        cost_estimate=pl.CostEstimate(
            flops=2 * occ * occ * TS**4, bytes_accessed=2 * TS**4, transcendentals=0
        ),
    )(arrived, ladder_ints)


def routes(members):
    lines = members // (SIDES * CORES)
    ring = list(range(0, lines, 2)) + list(range(1, lines, 2))[::-1]
    place = {line: n for n, line in enumerate(ring)}

    def member(line, side, core):
        return (line * SIDES + side) * CORES + core

    def split(t):
        return t // (SIDES * CORES), t // CORES % SIDES, t % CORES

    def behind(t, step):
        line, side, core = split(t)
        back = step if core == 0 else -step
        return member(ring[(place[line] - back) % lines], side, core)

    def across(t):
        line, side, core = split(t)
        return member(line, (side + 1) % SIDES, core)

    def beside(t):
        line, side, core = split(t)
        return member(line, side, (core + 1) % CORES)

    every = range(members)
    moves = {
        "ahead": [(behind(t, 1), t) for t in every],
        "back": [(behind(t, -1), t) for t in every],
        "over": [(across(t), t) for t in every],
        "pair": [(beside(t), t) for t in every],
    }
    return moves, {"ahead": lambda t: behind(t, 1), "back": lambda t: behind(t, -1), "over": across, "pair": beside}


class Gather:
    def __init__(self, block, members):
        self.members = members
        self.lines = members // (SIDES * CORES)
        self.moves, self.source = routes(members)
        self.blocks = [(block, list(range(members)), ("ahead", "back", "over", "pair"), 0)]
        self.fresh = list(self.blocks)

    def move(self, item, kind):
        block, owners, _, hops = item
        source = self.source[kind]
        new_owners = [owners[source(t)] for t in range(self.members)]
        follow = {"ahead": ("ahead", "over", "pair"), "back": ("back", "over", "pair"), "over": ("pair",), "pair": ()}[kind]
        hops = hops + 1 if kind in ("ahead", "back") else hops
        limit = {"ahead": self.lines // 2, "back": (self.lines - 1) // 2}
        follow = tuple(k for k in follow if hops < limit.get(k, hops + 1))
        return lax.ppermute(block, "tile", self.moves[kind]), new_owners, follow, hops

    def round(self):
        new = []
        for kind in ("ahead", "back", "over", "pair"):
            for item in self.fresh:
                if kind in item[2]:
                    new.append(self.move(item, kind))
        self.blocks += new
        self.fresh = new

    def tie(self, value):
        held = [item[0] for item in self.fresh]
        value, held = lax.optimization_barrier((value, held))
        tied = [(block,) + item[1:] for block, item in zip(held, self.fresh)]
        self.blocks[len(self.blocks) - len(tied):] = tied
        self.fresh = tied
        return value

    def places(self):
        table = np.array([item[1] for item in self.blocks], np.int32).T
        return lax.dynamic_index_in_dim(jnp.asarray(table), lax.axis_index("tile"), 0, keepdims=False)


def per_device(amps, ladder_ints, quad_pairs, cycle_ints):
    members = lax.axis_size("tile")
    occ = amps.shape[1]
    swap = functools.partial(lax.all_to_all, axis_name="tile", tiled=True)
    rows = Gather(cycle_ints, members)
    tags = jnp.broadcast_to(
        jnp.repeat(quad_pairs.astype(jnp.bfloat16), LANES // 2, axis=1)[:, None, :],
        (occ, NTP, LANES),
    )
    sent = jnp.concatenate([amps[0], tags], axis=2)
    rows.round()
    moved = rows.tie(swap(sent, split_axis=0, concat_axis=0))
    pairs = moved[:, 0, TS * TS:].astype(jnp.int32)
    targets, inputs = pairs[:, 0], pairs[:, LANES // 2]
    amp_cycle = moved[:, :, :TS * TS].transpose(1, 0, 2)
    tiles = amps[0].transpose(1, 0, 2)
    wanted = jnp.take(tiles, inputs, axis=0, mode="clip")
    rows.round()
    arrived = rows.tie(swap(wanted, split_axis=0, concat_axis=0))
    partial_value = ladder_partial(arrived, ladder_ints)
    rows.round()
    part_moved = rows.tie(swap(partial_value, split_axis=0, concat_axis=0))
    while rows.fresh:
        rows.round()
    pieces = [item[0] for item in rows.blocks]
    residual = finish(rows.places(), targets, part_moved, amp_cycle, pieces)
    return residual[:, None]


def solution(mesh):
    return jax.shard_map(
        per_device,
        mesh=mesh,
        in_specs=(
            P(("frag", "tile"), None, None, None),
            P(("frag", "tile"), None, None),
            P(("frag", "tile"), None),
            P(("frag", "tile"), None),
        ),
        out_specs=P("frag", "tile", None, None),
        check_vma=False,
    )
```

```python
import functools

import jax
import jax.numpy as jnp
import numpy as np
from jax import lax
from jax.experimental import pallas as pl
from jax.experimental.pallas import tpu as pltpu
from jax.sharding import PartitionSpec as P

TS = 32
VT = 4
NTP = VT * VT
LANES = 128
GROUPS = LANES // TS
STRIPES = TS // GROUPS
SIDES = 2
CORES = 2
MIB = 1024 * 1024

VMEM = pl.BlockSpec(memory_space=pltpu.VMEM)
SMEM = pl.BlockSpec(memory_space=pltpu.SMEM)


def swap_groups(four):
    lane = lax.broadcasted_iota(jnp.int32, four[0].shape, four[0].ndim - 1)
    low = lane < 2 * TS
    even = (lane // TS) % 2 == 0
    v = list(four)
    for p in (0, 1):
        a, b = v[p], v[p + 2]
        v[p] = jnp.where(low, a, pltpu.roll(b, 2 * TS, 1))
        v[p + 2] = jnp.where(low, pltpu.roll(a, 2 * TS, 1), b)
    for p in (0, 2):
        a, b = v[p], v[p + 1]
        v[p] = jnp.where(even, a, pltpu.roll(b, TS, 1))
        v[p + 1] = jnp.where(even, pltpu.roll(a, LANES - TS, 1), b)
    return v


def stripe(h):
    return slice(h * LANES, (h + 1) * LANES)


def ladder_kernel(arrived_ref, ints_ref, amps_ref, out_ref, total):
    occ = out_ref.shape[0]
    out_ref[:, occ:, :] = amps_ref[0]
    value = jnp.dot(
        arrived_ref[...].reshape(occ * occ, TS * TS),
        ints_ref[0],
        preferred_element_type=jnp.float32,
    )
    for h in range(STRIPES):
        total[h] = value[:, stripe(h)]
        for j in range(occ):
            rows = total[h, pl.ds(j, occ, stride=occ), :]
            out_ref[j, :occ, stripe(h)] = rows.astype(jnp.bfloat16)


def ladder_partial(arrived, ladder_ints, amps):
    occ = arrived.shape[0]
    return pl.pallas_call(
        ladder_kernel,
        out_shape=jax.ShapeDtypeStruct((occ, occ + NTP, TS * TS), jnp.bfloat16),
        in_specs=[VMEM] * 3,
        out_specs=VMEM,
        scratch_shapes=[pltpu.VMEM((STRIPES, occ * occ, LANES), jnp.float32)],
        compiler_params=pltpu.CompilerParams(vmem_limit_bytes=24 * MIB),
        cost_estimate=pl.CostEstimate(
            flops=2 * occ * occ * TS**4, bytes_accessed=2 * TS**4, transcendentals=0
        ),
    )(arrived, ladder_ints, amps)


def finish_kernel(me, table, targets, moved_ref, *rest):
    count = len(rest) - 5
    pieces = rest[:count]
    out_ref, ladder, columns, product, result = rest[count:]
    occ = out_ref.shape[0]
    if occ == NTP:
        for q in range(occ):
            ladder[targets[q]] = moved_ref[q, :occ].astype(jnp.float32)
    else:
        ladder[...] = jnp.zeros_like(ladder)
        for q in range(occ):
            ladder[targets[q]] += moved_ref[q, :occ].astype(jnp.float32)
    for h in range(STRIPES):
        wide = moved_ref[:, occ:, stripe(h)].astype(jnp.float32)
        result[h] = wide.reshape(occ * NTP, LANES)
    for C in range(VT):
        for h in range(STRIPES):
            four = []
            for B in range(VT):
                pair = C * VT + B
                amp = result[h, pl.ds(pair, occ, stride=NTP), :]
                four.append(amp + ladder[pair, :, stripe(h)])
            for g, value in enumerate(swap_groups(four)):
                columns[pl.ds(C * TS + h * GROUPS + g, occ, stride=VT * TS), :] = value
    right = columns[...].astype(jnp.bfloat16)

    for n, piece in enumerate(pieces):
        rows = piece.shape[0]
        start = pl.multiple_of(table[me[0], n] * rows, rows)
        product[pl.ds(start, rows), :] = jnp.dot(
            piece[...], right, preferred_element_type=jnp.float32
        )

    for h in range(STRIPES):
        for A in range(VT):
            four = [
                product[pl.ds(A * TS + h * GROUPS + g, occ, stride=VT * TS), :]
                for g in range(GROUPS)
            ]
            for B, value in enumerate(swap_groups(four)):
                pair = A * VT + B
                total = value + ladder[pair, :, stripe(h)]
                result[h, pl.ds(pair, occ, stride=NTP), :] = total
        out_ref[:, :, stripe(h)] = result[h].astype(jnp.bfloat16).reshape(occ, NTP, LANES)


def finish(me, table, targets, moved, pieces):
    occ = moved.shape[0]
    rows = occ * VT * TS
    return pl.pallas_call(
        finish_kernel,
        out_shape=jax.ShapeDtypeStruct((occ, NTP, TS * TS), jnp.bfloat16),
        in_specs=[SMEM] * 3 + [VMEM] * (1 + len(pieces)),
        out_specs=VMEM,
        scratch_shapes=[
            pltpu.VMEM((NTP, occ, TS * TS), jnp.float32),
            pltpu.VMEM((rows, LANES), jnp.float32),
            pltpu.VMEM((rows, LANES), jnp.float32),
            pltpu.VMEM((STRIPES, occ * NTP, LANES), jnp.float32),
        ],
        compiler_params=pltpu.CompilerParams(vmem_limit_bytes=52 * MIB),
        cost_estimate=pl.CostEstimate(
            flops=2 * rows * rows * LANES, bytes_accessed=2 * rows * rows, transcendentals=0
        ),
    )(me, table, targets, moved, *pieces)


class Rows:
    def __init__(self, array, owners):
        self.array, self.owners = array, owners

    def moved(self, targets):
        perm = sorted(targets.items())
        owners = [0] * len(self.owners)
        for source, target in perm:
            owners[target] = self.owners[source]
        return Rows(lax.ppermute(self.array, "tile", perm), owners)


def choose(mask, yes, no):
    mine = jnp.asarray(np.array(mask, np.int32))[lax.axis_index("tile")] == 1
    owners = [y if m else n for m, y, n in zip(mask, yes.owners, no.owners)]
    return Rows(jnp.where(mine, yes.array, no.array), owners)


def member(line, side, core):
    return (line * SIDES + side) * CORES + core


def split(t):
    return t // (SIDES * CORES), t // CORES % SIDES, t % CORES


def along_line(own, members):
    line = [split(t)[0] for t in range(members)]

    def hop(*pairs):
        ends = dict(pairs)
        return {t: member(ends[line[t]], *split(t)[1:]) for t in range(members) if line[t] in ends}

    inner = hop((1, 2), (2, 1))
    outward = hop((1, 0), (2, 3))
    outer = [n in (0, 3) for n in line]
    first = own.moved(hop((0, 1), (1, 0), (2, 3), (3, 2)))
    third_in = own.moved(inner)
    second_in = first.moved(inner)
    second_out = third_in.moved(outward)
    third_out = second_in.moved(outward)
    near = [own, first, choose(outer, second_out, second_in), choose(outer, third_out, third_in)]
    return near, [second_in]


def along_ring(own, members):
    lines = members // (SIDES * CORES)
    ring = list(range(0, lines, 2)) + list(range(1, lines, 2))[::-1]
    place = {n: p for p, n in enumerate(ring)}

    def turn(step):
        targets = {}
        for t in range(members):
            line, side, core = split(t)
            ahead = step if core == 0 else -step
            targets[t] = member(ring[(place[line] + ahead) % lines], side, core)
        return targets

    blocks = [own]
    for step, count in ((1, lines // 2), (-1, (lines - 1) // 2)):
        last = own
        for _ in range(count):
            last = last.moved(turn(step))
            blocks.append(last)
    return blocks, []


def wait_for(value, blocks):
    return lax.optimization_barrier((value, [block.array for block in blocks]))[0]


def per_device(amps, ladder_ints, quad_pairs, cycle_ints):
    members = lax.axis_size("tile")
    swap = functools.partial(
        lax.all_to_all, axis_name="tile", split_axis=0, concat_axis=0, tiled=True
    )

    own = Rows(cycle_ints, list(range(members)))
    lines = members // (SIDES * CORES)
    near, soon = (along_line if lines == 4 else along_ring)(own, members)
    side = {t: member(split(t)[0], (split(t)[1] + 1) % SIDES, split(t)[2]) for t in range(members)}
    core = {t: member(*split(t)[:2], (split(t)[2] + 1) % CORES) for t in range(members)}
    over = [block.moved(side) for block in near]
    blocks = near + over
    blocks += [block.moved(core) for block in blocks]
    table = np.array([block.owners for block in blocks], np.int32).T
    me = lax.axis_index("tile").astype(jnp.int32)[None]

    pairs = swap(jnp.broadcast_to(quad_pairs, (members, 2)))
    targets, inputs = pairs[:, 0], pairs[:, 1]
    tiles = amps[0].transpose(1, 0, 2)
    wanted = wait_for(jnp.take(tiles, inputs, axis=0, mode="clip"), over[:1])
    arrived = swap(wanted)
    sent = wait_for(ladder_partial(arrived, ladder_ints, amps), over[1:2] + soon)
    moved = swap(sent)
    residual = finish(me, table, targets, moved, [block.array for block in blocks])
    return residual[:, None]


def solution(mesh):
    return jax.shard_map(
        per_device,
        mesh=mesh,
        in_specs=(
            P(("frag", "tile"), None, None, None),
            P(("frag", "tile"), None, None),
            P(("frag", "tile"), None),
            P(("frag", "tile"), None),
        ),
        out_specs=P("frag", "tile", None, None),
        check_vma=False,
    )
```

```python
import functools

import jax
import jax.numpy as jnp
import numpy as np
from jax import lax
from jax.experimental import pallas as pl
from jax.experimental.pallas import tpu as pltpu
from jax.sharding import PartitionSpec as P

TS = 32
VT = 4
NTP = VT * VT
AHEAD = NTP // 2
LANES = 128
GROUPS = LANES // TS
STRIPES = TS // GROUPS
SIDES = 2
CORES = 2
MIB = 1024 * 1024

VMEM = pl.BlockSpec(memory_space=pltpu.VMEM)
SMEM = pl.BlockSpec(memory_space=pltpu.SMEM)


def swap_groups(four):
    lane = lax.broadcasted_iota(jnp.int32, four[0].shape, four[0].ndim - 1)
    low = lane < 2 * TS
    even = (lane // TS) % 2 == 0
    v = list(four)
    for p in (0, 1):
        a, b = v[p], v[p + 2]
        v[p] = jnp.where(low, a, pltpu.roll(b, 2 * TS, 1))
        v[p + 2] = jnp.where(low, pltpu.roll(a, 2 * TS, 1), b)
    for p in (0, 2):
        a, b = v[p], v[p + 1]
        v[p] = jnp.where(even, a, pltpu.roll(b, TS, 1))
        v[p + 1] = jnp.where(even, pltpu.roll(a, LANES - TS, 1), b)
    return v


def stripe(h):
    return slice(h * LANES, (h + 1) * LANES)


def ladder_kernel(arrived_ref, ints_ref, amps_ref, out_ref, total):
    occ = out_ref.shape[0]
    out_ref[:, occ:, :] = amps_ref[0, :, AHEAD:, :]
    value = jnp.dot(
        arrived_ref[...].reshape(occ * occ, TS * TS),
        ints_ref[0],
        preferred_element_type=jnp.float32,
    )
    for h in range(STRIPES):
        total[h] = value[:, stripe(h)]
        for j in range(occ):
            rows = total[h, pl.ds(j, occ, stride=occ), :]
            out_ref[j, :occ, stripe(h)] = rows.astype(jnp.bfloat16)


def ladder_partial(arrived, ladder_ints, amps):
    occ = arrived.shape[0]
    return pl.pallas_call(
        ladder_kernel,
        out_shape=jax.ShapeDtypeStruct((occ, occ + NTP - AHEAD, TS * TS), jnp.bfloat16),
        in_specs=[VMEM] * 3,
        out_specs=VMEM,
        scratch_shapes=[pltpu.VMEM((STRIPES, occ * occ, LANES), jnp.float32)],
        compiler_params=pltpu.CompilerParams(vmem_limit_bytes=24 * MIB),
        cost_estimate=pl.CostEstimate(
            flops=2 * occ * occ * TS**4, bytes_accessed=2 * TS**4, transcendentals=0
        ),
    )(arrived, ladder_ints, amps)


def finish_kernel(me, table, targets, ahead_ref, moved_ref, *rest):
    count = len(rest) - 5
    pieces = rest[:count]
    out_ref, ladder, columns, product, result = rest[count:]
    occ = out_ref.shape[0]
    if occ == NTP:
        for q in range(occ):
            ladder[targets[q]] = moved_ref[q, :occ].astype(jnp.float32)
    else:
        ladder[...] = jnp.zeros_like(ladder)
        for q in range(occ):
            ladder[targets[q]] += moved_ref[q, :occ].astype(jnp.float32)
    for h in range(STRIPES):
        halves = [ahead_ref[:, :, stripe(h)], moved_ref[:, occ:, stripe(h)]]
        wide = jnp.concatenate([half.astype(jnp.float32) for half in halves], axis=1)
        result[h] = wide.reshape(occ * NTP, LANES)
    for C in range(VT):
        for h in range(STRIPES):
            four = []
            for B in range(VT):
                pair = C * VT + B
                amp = result[h, pl.ds(pair, occ, stride=NTP), :]
                four.append(amp + ladder[pair, :, stripe(h)])
            for g, value in enumerate(swap_groups(four)):
                columns[pl.ds(C * TS + h * GROUPS + g, occ, stride=VT * TS), :] = value
    right = columns[...].astype(jnp.bfloat16)

    for n, piece in enumerate(pieces):
        rows = piece.shape[0]
        start = pl.multiple_of(table[me[0], n] * rows, rows)
        product[pl.ds(start, rows), :] = jnp.dot(
            piece[...], right, preferred_element_type=jnp.float32
        )

    for h in range(STRIPES):
        for A in range(VT):
            four = [
                product[pl.ds(A * TS + h * GROUPS + g, occ, stride=VT * TS), :]
                for g in range(GROUPS)
            ]
            for B, value in enumerate(swap_groups(four)):
                pair = A * VT + B
                total = value + ladder[pair, :, stripe(h)]
                result[h, pl.ds(pair, occ, stride=NTP), :] = total
        out_ref[:, :, stripe(h)] = result[h].astype(jnp.bfloat16).reshape(occ, NTP, LANES)


def finish(me, table, targets, ahead, moved, pieces):
    occ = moved.shape[0]
    rows = occ * VT * TS
    return pl.pallas_call(
        finish_kernel,
        out_shape=jax.ShapeDtypeStruct((occ, NTP, TS * TS), jnp.bfloat16),
        in_specs=[SMEM] * 3 + [VMEM] * (2 + len(pieces)),
        out_specs=VMEM,
        scratch_shapes=[
            pltpu.VMEM((NTP, occ, TS * TS), jnp.float32),
            pltpu.VMEM((rows, LANES), jnp.float32),
            pltpu.VMEM((rows, LANES), jnp.float32),
            pltpu.VMEM((STRIPES, occ * NTP, LANES), jnp.float32),
        ],
        compiler_params=pltpu.CompilerParams(vmem_limit_bytes=52 * MIB),
        cost_estimate=pl.CostEstimate(
            flops=2 * rows * rows * LANES, bytes_accessed=2 * rows * rows, transcendentals=0
        ),
    )(me, table, targets, ahead, moved, *pieces)


class Rows:
    def __init__(self, array, owners):
        self.array, self.owners = array, owners

    def moved(self, targets):
        perm = sorted(targets.items())
        owners = [0] * len(self.owners)
        for source, target in perm:
            owners[target] = self.owners[source]
        return Rows(lax.ppermute(self.array, "tile", perm), owners)


def choose(mask, yes, no):
    mine = jnp.asarray(np.array(mask, np.int32))[lax.axis_index("tile")] == 1
    owners = [y if m else n for m, y, n in zip(mask, yes.owners, no.owners)]
    return Rows(jnp.where(mine, yes.array, no.array), owners)


def member(line, side, core):
    return (line * SIDES + side) * CORES + core


def split(t):
    return t // (SIDES * CORES), t // CORES % SIDES, t % CORES


def along_line(own, members):
    line = [split(t)[0] for t in range(members)]

    def hop(*pairs):
        ends = dict(pairs)
        return {t: member(ends[line[t]], *split(t)[1:]) for t in range(members) if line[t] in ends}

    inner = hop((1, 2), (2, 1))
    outward = hop((1, 0), (2, 3))
    outer = [n in (0, 3) for n in line]
    first = own.moved(hop((0, 1), (1, 0), (2, 3), (3, 2)))
    third_in = own.moved(inner)
    second_in = first.moved(inner)
    second_out = third_in.moved(outward)
    third_out = second_in.moved(outward)
    near = [own, first, choose(outer, second_out, third_in), choose(outer, third_out, second_in)]
    return near, [second_in]


def along_ring(own, members):
    lines = members // (SIDES * CORES)
    ring = list(range(0, lines, 2)) + list(range(1, lines, 2))[::-1]
    place = {n: p for p, n in enumerate(ring)}

    def turn(step):
        targets = {}
        for t in range(members):
            line, side, core = split(t)
            ahead = step if core == 0 else -step
            targets[t] = member(ring[(place[line] + ahead) % lines], side, core)
        return targets

    blocks = [own]
    for step, count in ((1, lines // 2), (-1, (lines - 1) // 2)):
        last = own
        for _ in range(count):
            last = last.moved(turn(step))
            blocks.append(last)
    return blocks, []


def wait_for(value, blocks):
    return lax.optimization_barrier((value, [block.array for block in blocks]))[0]


def per_device(amps, ladder_ints, quad_pairs, cycle_ints):
    members = lax.axis_size("tile")
    swap = functools.partial(
        lax.all_to_all, axis_name="tile", split_axis=0, concat_axis=0, tiled=True
    )

    own = Rows(cycle_ints, list(range(members)))
    lines = members // (SIDES * CORES)
    near, soon = (along_line if lines == 4 else along_ring)(own, members)
    side = {t: member(split(t)[0], (split(t)[1] + 1) % SIDES, split(t)[2]) for t in range(members)}
    core = {t: member(*split(t)[:2], (split(t)[2] + 1) % CORES) for t in range(members)}
    over = [block.moved(side) for block in near]
    blocks = near + over
    blocks += [block.moved(core) for block in blocks]
    table = np.array([block.owners for block in blocks], np.int32).T
    me = lax.axis_index("tile").astype(jnp.int32)[None]

    tags = jnp.repeat(quad_pairs.astype(jnp.bfloat16), LANES // 2, axis=1)[:, None, :]
    tags = jnp.broadcast_to(tags, (members, AHEAD, LANES))
    ahead = swap(jnp.concatenate([amps[0, :, :AHEAD], tags], axis=2))
    pairs = ahead[:, 0, TS * TS:].astype(jnp.int32)
    targets, inputs = pairs[:, 0], pairs[:, LANES // 2]
    tiles = amps[0].transpose(1, 0, 2)
    wanted = wait_for(jnp.take(tiles, inputs, axis=0, mode="clip"), over[:1])
    arrived = swap(wanted)
    sent = wait_for(ladder_partial(arrived, ladder_ints, amps), over[1:2] + soon)
    moved = swap(sent)
    residual = finish(me, table, targets, ahead, moved, [block.array for block in blocks])
    return residual[:, None]


def solution(mesh):
    return jax.shard_map(
        per_device,
        mesh=mesh,
        in_specs=(
            P(("frag", "tile"), None, None, None),
            P(("frag", "tile"), None, None),
            P(("frag", "tile"), None),
            P(("frag", "tile"), None),
        ),
        out_specs=P("frag", "tile", None, None),
        check_vma=False,
    )
```
